32 devices in a mesh: groups: 2 (over y), walker: 16 (over z, x, core).
Axes of the slice: x: 2, y: 2, z: 4, core: 2. Of those that a mesh axis runs over, the one named last changes fastest.
Arguments:
- log_grads: float32 [256, 2048], P(('groups', 'walker')), parts along dimension 0
- local_energy: float32 [256], P(('groups', 'walker')), parts along dimension 0
- prev_update: float32 [4096], P('groups'), parts along dimension 0, may hold values from -6 to 6
Outputs:
- kernel_rows: float32 [256, 128], P(('groups', 'walker')), parts along dimension 0
- coeffs: float32 [256], P(('groups', 'walker')), parts along dimension 0
- update: float32 [4096], P('groups'), parts along dimension 0
The draws below stay inside these ranges and needn't reach their ends.
There are 2 independent parts, one for each index of `groups`. The reference program is written for one: setup_inputs(seed, part) draws one part's arguments, and reference() takes and returns one part's arrays. A program takes and returns all parts, laid end to end along the dimension named above; each array names one. Nothing has to cross between parts.
All inputs are finite; a program needn't handle non-finite values.
Results may differ from the reference program's by a relative error of at most 0.0015.
Values may be sent and summed in bfloat16 or wider, within the bound.
A program may use at most 64 MiB of HBM per device.

```python
import jax
import jax.numpy as jnp
from jax import lax

P_SIZE = 2048
ITERS = 2
NW = 128


def draw_log_grads(key, part):
    key = jax.random.fold_in(key, 11)
    k_base, k_col, k_row, k_off = jax.random.split(key, 4)
    rise = 1.0 + 2.0 * jnp.arange(NW, dtype=jnp.float32)[:, None] / NW
    row = rise * jnp.exp(jax.random.uniform(k_row, (NW, 1), minval=0.0, maxval=0.7))
    base = jax.random.normal(k_base, (NW, P_SIZE))
    column = jnp.exp(jax.random.uniform(k_col, (1, P_SIZE), minval=-1.2, maxval=1.2))
    shift = 0.5
    offset = jax.random.normal(k_off, (1, P_SIZE)) * shift
    return ((base * row + offset) * column).astype(jnp.float32)


def draw_local_energy(key, part):
    key = jax.random.fold_in(key, 23)
    rise = 1.0 + 2.0 * jnp.arange(NW, dtype=jnp.float32) / NW
    base = jax.random.normal(key, (NW,))
    offset = 1.5
    return (base * rise + offset).astype(jnp.float32)


def scatter_about(own_key, dims, width, most, kind=jnp.bfloat16):
    entries = jax.random.normal(own_key, dims, jnp.float32) * width
    return jnp.minimum(jnp.maximum(entries, -most), most).astype(kind)


def setup_inputs(seed: int = 0, part: int = 0) -> dict:
    splits = jax.random.split(jax.random.key(seed), 4)
    own_keys = jax.random.split(jax.random.fold_in(splits[3], part), 4)
    return {
        "log_grads": draw_log_grads(jax.random.fold_in(jax.random.fold_in(splits[3], part), 71), part),
        "local_energy": draw_local_energy(jax.random.fold_in(jax.random.fold_in(splits[3], part), 71), part),
        "prev_update": scatter_about(own_keys[2], (P_SIZE,), 1.0, 6.0, jnp.float32),
    }


momentum = 0.9
damping = 0.5


def reference(log_grads, local_energy, prev_update):
    count = log_grads.shape[0]
    high = lax.Precision.HIGHEST
    mean_grad = jnp.sum(log_grads, axis=0) / count
    energy_mean = jnp.sum(local_energy) / count
    centered = (log_grads - mean_grad) * (count ** -0.5)
    blocks = centered.astype(jnp.bfloat16).astype(jnp.float32)
    kernel_rows = jnp.dot(blocks, blocks.T, precision=high)
    target = -(local_energy - energy_mean) - momentum * jnp.dot(centered, prev_update, precision=high)
    coeffs = jnp.zeros_like(target)
    residual = target
    direction = target
    norm_now = jnp.sum(residual * residual)
    for step in range(ITERS):
        image = jnp.dot(kernel_rows, direction, precision=high) + damping * direction
        alpha = norm_now / jnp.sum(direction * image)
        coeffs = coeffs + alpha * direction
        residual = residual - alpha * image
        norm_next = jnp.sum(residual * residual)
        direction = residual + (norm_next / norm_now) * direction
        norm_now = norm_next
    update = jnp.dot(coeffs, centered, precision=high) + momentum * prev_update
    return kernel_rows, coeffs, update
```

```python
import functools

import jax
import jax.numpy as jnp
from jax import lax
from jax.experimental import pallas as pl
from jax.experimental.pallas import tpu as pltpu
from jax.sharding import PartitionSpec as P

ITERS = 2
LANES = 128
ROWS = 8
MESH = pl.DeviceIdType.MESH

momentum = 0.9
damping = 0.5


def kernel(
    n, x_hbm, e_hbm, p_hbm, rows_ref, coeffs_ref, update_ref,
    x_ref, e_ref, p_ref, tiles, w_rows, y_rows, k_send, k_recv, fin,
    in_sem, send_sem, recv_sem,
):
    walkers = n * ROWS
    scale = walkers ** (-0.5)
    group = lax.axis_index("groups")
    me = lax.axis_index("walker")
    peers = [lax.rem(me + k, n) for k in range(n - 1, 0, -1)]

    barrier = pltpu.get_barrier_semaphore()
    for peer in peers:
        pl.semaphore_signal(barrier, inc=1, device_id=(group, peer), device_id_type=MESH)
    loads = [
        pltpu.make_async_copy(x_hbm, x_ref, in_sem.at[0]),
        pltpu.make_async_copy(p_hbm, p_ref, in_sem.at[1]),
        pltpu.make_async_copy(e_hbm, e_ref, in_sem.at[2]),
    ]
    for load in loads:
        load.start()
    for load in loads:
        load.wait()

    def column_tile(peer):
        return x_ref.at[:, pl.ds(pl.multiple_of(peer * LANES, LANES), LANES)]

    def remote(src, dst, which, peer):
        return pltpu.make_async_remote_copy(
            src_ref=src, dst_ref=dst, send_sem=send_sem.at[which], recv_sem=recv_sem.at[which],
            device_id=(group, peer), device_id_type=MESH,
        )

    def arrived(ref, which):
        part = ref.at[pl.ds(0, n - 1)]
        pltpu.make_async_copy(part, part, recv_sem.at[which]).wait()

    def sent(ref, which):
        part = ref.at[pl.ds(0, n - 1)]
        pltpu.make_async_copy(part, part, send_sem.at[which]).wait()

    lane = lax.broadcasted_iota(jnp.int32, (1, LANES), 1)
    lane8 = lax.broadcasted_iota(jnp.int32, (ROWS, LANES), 1)
    sub8 = lax.broadcasted_iota(jnp.int32, (ROWS, LANES), 0)

    acc = jnp.zeros((ROWS, LANES), jnp.float32)
    for k in range(n):
        acc = acc + x_ref[:, k * LANES : (k + 1) * LANES] * p_ref[k : k + 1, :]
    own = jnp.sum(acc, axis=1, keepdims=True) * (-momentum * scale)
    w_row = jnp.sum(jnp.where(lane8 == me * ROWS + sub8, own, 0.0), axis=0, keepdims=True)
    for i in range(ROWS):
        w_row = w_row - jnp.where(lane == me * ROWS + i, e_ref[i], 0.0)
    w_rows[me] = w_row
    tiles[me] = x_ref[:, pl.ds(pl.multiple_of(me * LANES, LANES), LANES)]

    pl.semaphore_wait(barrier, n - 1)
    for peer in peers:
        remote(column_tile(peer), tiles.at[me], 0, peer).start()
        remote(w_rows.at[me], w_rows.at[me], 1, peer).start()

    sub = lax.broadcasted_iota(jnp.int32, (walkers, LANES), 0)
    lanes = lax.broadcasted_iota(jnp.int32, (walkers, LANES), 1)
    diagonal = sub == lanes

    def to_column(row):
        return jnp.sum(jnp.where(diagonal, row, 0.0), axis=1, keepdims=True)

    def to_row(column):
        return jnp.sum(jnp.where(diagonal, column, 0.0), axis=0, keepdims=True)

    arrived(w_rows, 1)
    w = jnp.sum(w_rows[...], axis=0)
    t = w - jnp.sum(w, axis=1, keepdims=True) / walkers
    t_col = to_column(t)
    arrived(tiles, 0)
    x = tiles[...].reshape(walkers, LANES)
    centered = (x - jnp.sum(x, axis=0, keepdims=True) / walkers) * scale
    half = centered.astype(jnp.bfloat16)
    blocks = half.astype(jnp.float32)
    bt = jnp.sum(blocks * t_col, axis=0, keepdims=True)
    y_rows[me] = to_row(jnp.sum(blocks * bt, axis=1, keepdims=True))
    for peer in peers:
        remote(y_rows.at[me], y_rows.at[me], 2, peer).start()

    k_part = lax.dot_general(half, half, (((1,), (1,)), ((), ())), preferred_element_type=jnp.float32)
    k_send[...] = k_part.reshape(n, ROWS, LANES)
    k_recv[me] = k_send[me]
    for peer in peers:
        remote(k_send.at[peer], k_recv.at[me], 3, peer).start()
    ct = jnp.sum(centered * t_col, axis=0, keepdims=True)
    norm = jnp.sum(t * t, axis=1, keepdims=True)

    arrived(y_rows, 2)
    image = jnp.sum(y_rows[...], axis=0) + damping * t
    alpha = norm / jnp.sum(t * image, axis=1, keepdims=True)
    residual = t - alpha * image
    norm_next = jnp.sum(residual * residual, axis=1, keepdims=True)
    direction = residual + norm_next / norm * t
    d_col = to_column(direction)
    bd = jnp.sum(blocks * d_col, axis=0, keepdims=True)
    cd = jnp.sum(centered * d_col, axis=0, keepdims=True)
    fin[me, :, 0:LANES] = alpha * ct + momentum * p_ref[pl.ds(me, 1), :]
    fin[me, :, LANES : 2 * LANES] = cd
    fin[me, :, 2 * LANES : 3 * LANES] = bd * bd
    for peer in peers:
        remote(fin.at[me], fin.at[me], 4, peer).start()

    square = jnp.sum(direction * direction, axis=1, keepdims=True)
    arrived(k_recv, 3)
    rows_ref[...] = jnp.sum(k_recv[...], axis=0)

    arrived(fin, 4)
    curve = jnp.sum(jnp.sum(fin[:, :, 2 * LANES : 3 * LANES], axis=0), axis=1, keepdims=True)
    alpha2 = norm_next / (curve + damping * square)
    coeffs = alpha * t + alpha2 * direction
    coeffs_ref[...] = jnp.broadcast_to(
        jnp.sum(jnp.where(lane8 == me * ROWS + sub8, coeffs, 0.0), axis=1, keepdims=True), (ROWS, LANES)
    )
    for k in range(n):
        update_ref[k : k + 1, :] = fin[k, :, 0:LANES] + alpha2 * fin[k, :, LANES : 2 * LANES]

    sent(tiles, 0)
    sent(w_rows, 1)
    sent(y_rows, 2)
    sent(k_recv, 3)
    sent(fin, 4)


def fused(log_grads, local_energy, prev_update):
    n = lax.axis_size("walker")
    f32 = jnp.float32
    rows, coeffs, update = pl.pallas_call(
        functools.partial(kernel, n),
        out_shape=(
            jax.ShapeDtypeStruct((ROWS, LANES), f32),
            jax.ShapeDtypeStruct((ROWS, LANES), f32),
            jax.ShapeDtypeStruct((n, LANES), f32),
        ),
        in_specs=[pl.BlockSpec(memory_space=pl.ANY)] * 3,
        out_specs=[pl.BlockSpec(memory_space=pltpu.VMEM)] * 3,
        scratch_shapes=[
            pltpu.VMEM((ROWS, n * LANES), f32),
            pltpu.SMEM((ROWS,), f32),
            pltpu.VMEM((n, LANES), f32),
            pltpu.VMEM((n, ROWS, LANES), f32),
            pltpu.VMEM((n, 1, LANES), f32),
            pltpu.VMEM((n, 1, LANES), f32),
            pltpu.VMEM((n, ROWS, LANES), f32),
            pltpu.VMEM((n, ROWS, LANES), f32),
            pltpu.VMEM((n, 1, 3 * LANES), f32),
            pltpu.SemaphoreType.DMA((3,)),
            pltpu.SemaphoreType.DMA((5,)),
            pltpu.SemaphoreType.DMA((5,)),
        ],
        compiler_params=pltpu.CompilerParams(collective_id=0, has_side_effects=True),
    )(log_grads, local_energy, prev_update.reshape(n, LANES))
    return rows, coeffs[:, 0], update.reshape(n * LANES)


def plain(log_grads, local_energy, prev_update):
    high = lax.Precision.HIGHEST
    rows = log_grads.shape[0]
    count = rows * lax.axis_size("walker")
    col_sum, energy_sum = lax.psum((jnp.sum(log_grads, axis=0), jnp.sum(local_energy)), "walker")
    centered = (log_grads - col_sum / count) * count ** (-0.5)
    blocks = centered.astype(jnp.bfloat16)
    gathered = lax.all_gather(blocks, "walker", axis=0, tiled=True)
    kernel_rows = lax.dot_general(
        blocks, gathered, (((1,), (1,)), ((), ())), preferred_element_type=jnp.float32
    )
    target = -(local_energy - energy_sum / count) - momentum * jnp.dot(
        centered, prev_update, precision=high
    )
    coeffs = jnp.zeros_like(target)
    residual = target

    def squares(resid):
        return lax.psum(jnp.sum(resid * resid), "walker")

    direction = residual
    norm_now = squares(residual)
    for step in range(ITERS):
        full = lax.all_gather(direction, "walker", axis=0, tiled=True)
        image = jnp.dot(kernel_rows, full, precision=high) + damping * direction
        alpha = norm_now / lax.psum(jnp.sum(direction * image), "walker")
        coeffs = coeffs + alpha * direction
        if step + 1 < ITERS:
            residual = residual - alpha * image
            norm_next = squares(residual)
            direction = residual + norm_next / norm_now * direction
            norm_now = norm_next
    update = lax.psum(jnp.dot(coeffs, centered, precision=high), "walker") + momentum * prev_update
    return (kernel_rows, coeffs, update)


def local(log_grads, local_energy, prev_update):
    rows, columns = log_grads.shape
    n = lax.axis_size("walker")
    if rows == ROWS and n * ROWS == LANES and columns == n * LANES:
        return fused(log_grads, local_energy, prev_update)
    return plain(log_grads, local_energy, prev_update)


def solution(mesh):
    in_specs = (P(("groups", "walker"), None), P(("groups", "walker")), P("groups"))
    out_specs = (P(("groups", "walker"), None), P(("groups", "walker")), P("groups"))
    return jax.shard_map(local, mesh=mesh, in_specs=in_specs, out_specs=out_specs, check_vma=False)
```

```python
import functools

import jax
import jax.numpy as jnp
from jax import lax
from jax.experimental import pallas as pl
from jax.experimental.pallas import tpu as pltpu
from jax.sharding import PartitionSpec as P

ITERS = 2
LANES = 128
ROWS = 8
TEAM = 8
MESH = pl.DeviceIdType.MESH

momentum = 0.9
damping = 0.5


def kernel(
    n, m, x_hbm, e_hbm, p_hbm, rows_ref, coeffs_ref, update_ref,
    x_ref, e_ref, p_ref, tiles, w_rows, y_rows, k_send, k_recv, fin,
    in_sem, send_sem, recv_sem,
):
    walkers = n * ROWS
    width = tiles.shape[2]
    chunks = width // LANES
    scale = walkers ** (-0.5)
    group = lax.axis_index("groups")
    me = lax.axis_index("walker")
    pos = lax.rem(me, m)
    team = me - pos
    peers = [lax.rem(me + k, n) for k in range(n - 1, 0, -1)]
    mates = [lax.rem(pos + k, m) for k in range(m - 1, 0, -1)]

    barrier = pltpu.get_barrier_semaphore()
    for peer in peers:
        pl.semaphore_signal(barrier, inc=1, device_id=(group, peer), device_id_type=MESH)
    loads = [
        pltpu.make_async_copy(x_hbm, x_ref, in_sem.at[0]),
        pltpu.make_async_copy(p_hbm, p_ref, in_sem.at[1]),
        pltpu.make_async_copy(e_hbm, e_ref, in_sem.at[2]),
    ]
    for load in loads:
        load.start()
    for load in loads:
        load.wait()

    def share(place):
        return pl.ds(pl.multiple_of(place * width, LANES), width)

    def remote(src, dst, which, peer):
        return pltpu.make_async_remote_copy(
            src_ref=src, dst_ref=dst, send_sem=send_sem.at[which], recv_sem=recv_sem.at[which],
            device_id=(group, peer), device_id_type=MESH,
        )

    def wait_all(ref, count, sem):
        if count:
            part = ref.at[pl.ds(0, count)]
            pltpu.make_async_copy(part, part, sem).wait()

    lane = lax.broadcasted_iota(jnp.int32, (1, LANES), 1)
    lane8 = lax.broadcasted_iota(jnp.int32, (ROWS, LANES), 1)
    sub8 = lax.broadcasted_iota(jnp.int32, (ROWS, LANES), 0)

    acc = jnp.zeros((ROWS, LANES), jnp.float32)
    for k in range(p_ref.shape[0]):
        acc = acc + x_ref[:, k * LANES : (k + 1) * LANES] * p_ref[k : k + 1, :]
    own = jnp.sum(acc, axis=1, keepdims=True) * (-momentum * scale)
    w_row = jnp.sum(jnp.where(lane8 == me * ROWS + sub8, own, 0.0), axis=0, keepdims=True)
    for i in range(ROWS):
        w_row = w_row - jnp.where(lane == me * ROWS + i, e_ref[i], 0.0)
    w_rows[me] = w_row
    tiles[me] = x_ref[:, share(pos)]

    pl.semaphore_wait(barrier, n - 1)
    for peer in peers:
        remote(w_rows.at[me], w_rows.at[me], 1, peer).start()
        remote(x_ref.at[:, share(lax.rem(peer, m))], tiles.at[me], 0, peer).start()

    sub = lax.broadcasted_iota(jnp.int32, (walkers, LANES), 0)
    lanes = lax.broadcasted_iota(jnp.int32, (walkers, LANES), 1)
    diagonal = sub == lanes

    def to_column(row):
        return jnp.sum(jnp.where(diagonal, row, 0.0), axis=1, keepdims=True)

    def to_row(column):
        return jnp.sum(jnp.where(diagonal, column, 0.0), axis=0, keepdims=True)

    def cols(c):
        return slice(c * LANES, (c + 1) * LANES)

    def rounded(c):
        return tiles[:, :, cols(c)].reshape(walkers, LANES).astype(jnp.bfloat16).astype(jnp.float32)

    wait_all(w_rows, n - 1, recv_sem.at[1])
    w = jnp.sum(w_rows[...], axis=0)
    t = w - jnp.sum(w, axis=1, keepdims=True) / walkers
    t_col = to_column(t)
    wait_all(tiles, n - 1, recv_sem.at[0])
    y_acc = jnp.zeros((walkers, LANES), jnp.float32)
    bt = []
    for c in range(chunks):
        x = tiles[:, :, cols(c)].reshape(walkers, LANES)
        centered = (x - jnp.sum(x, axis=0, keepdims=True) / walkers) * scale
        tiles[:, :, cols(c)] = centered.reshape(n, ROWS, LANES)
        blocks = centered.astype(jnp.bfloat16).astype(jnp.float32)
        bt.append(jnp.sum(blocks * t_col, axis=0, keepdims=True))
        y_acc = y_acc + blocks * bt[c]
    y_rows[pos] = to_row(jnp.sum(y_acc, axis=1, keepdims=True))
    for mate in mates:
        remote(y_rows.at[pos], y_rows.at[pos], 2, team + mate).start()

    half = tiles[...].reshape(walkers, width).astype(jnp.bfloat16)
    ours = tiles[pl.ds(team, m)].reshape(m * ROWS, width).astype(jnp.bfloat16)
    k_part = lax.dot_general(ours, half, (((1,), (1,)), ((), ())), preferred_element_type=jnp.float32)
    k_send[...] = k_part.reshape(m, ROWS, LANES)
    k_recv[pos] = k_send[pos]
    for mate in mates:
        remote(k_send.at[mate], k_recv.at[pos], 3, team + mate).start()
    ct = [
        jnp.sum(tiles[:, :, cols(c)].reshape(walkers, LANES) * t_col, axis=0, keepdims=True)
        for c in range(chunks)
    ]
    norm = jnp.sum(t * t, axis=1, keepdims=True)

    wait_all(y_rows, m - 1, recv_sem.at[2])
    image = jnp.sum(y_rows[...], axis=0) + damping * t
    i_col = to_column(image)
    alpha = norm / jnp.sum(t * image, axis=1, keepdims=True)
    residual = t - alpha * image
    norm_next = jnp.sum(residual * residual, axis=1, keepdims=True)
    beta = norm_next / norm
    direction = residual + beta * t
    squares = jnp.zeros((1, LANES), jnp.float32)
    for c in range(chunks):
        bi = jnp.sum(rounded(c) * i_col, axis=0, keepdims=True)
        ci = jnp.sum(tiles[:, :, cols(c)].reshape(walkers, LANES) * i_col, axis=0, keepdims=True)
        bd = (bt[c] - alpha * bi) + beta * bt[c]
        squares = squares + bd * bd
        fin[pos, :, cols(c)] = alpha * ct[c] + momentum * p_ref[pl.ds(pos * chunks + c, 1), :]
        fin[pos, :, cols(chunks + c)] = (ct[c] - alpha * ci) + beta * ct[c]
    fin[pos, :, cols(2 * chunks)] = squares
    for mate in mates:
        remote(fin.at[pos], fin.at[pos], 4, team + mate).start()

    square = jnp.sum(direction * direction, axis=1, keepdims=True)
    wait_all(k_recv, m - 1, recv_sem.at[3])
    rows_ref[...] = jnp.sum(k_recv[...], axis=0)

    wait_all(fin, m - 1, recv_sem.at[4])
    curve = jnp.sum(jnp.sum(fin[:, :, cols(2 * chunks)], axis=0), axis=1, keepdims=True)
    alpha2 = norm_next / (curve + damping * square)
    coeffs = alpha * t + alpha2 * direction
    coeffs_ref[...] = pltpu.roll(coeffs, lax.rem(walkers - me * ROWS, walkers), 1)
    for k in range(m * chunks):
        owner, c = k // chunks, k % chunks
        update_ref[k : k + 1, :] = fin[owner, :, cols(c)] + alpha2 * fin[owner, :, cols(chunks + c)]

    wait_all(tiles, n - 1, send_sem.at[0])
    wait_all(w_rows, n - 1, send_sem.at[1])
    wait_all(y_rows, m - 1, send_sem.at[2])
    wait_all(k_recv, m - 1, send_sem.at[3])
    wait_all(fin, m - 1, send_sem.at[4])


def finish(rows_in, coeffs_in, update_in, rows_ref, coeffs_ref, update_ref):
    rows_ref[...] = rows_in[...]
    coeffs_ref[...] = coeffs_in[0, 0:ROWS]
    update_ref[...] = update_in[...]


def fused(log_grads, local_energy, prev_update):
    n = lax.axis_size("walker")
    m = TEAM
    size = prev_update.shape[0]
    width = size // m
    f32 = jnp.float32
    rows, coeffs, update = pl.pallas_call(
        functools.partial(kernel, n, m),
        out_shape=(
            jax.ShapeDtypeStruct((ROWS, LANES), f32),
            jax.ShapeDtypeStruct((1, LANES), f32),
            jax.ShapeDtypeStruct((size // LANES, LANES), f32),
        ),
        in_specs=[pl.BlockSpec(memory_space=pl.ANY)] * 3,
        out_specs=[pl.BlockSpec(memory_space=pltpu.VMEM)] * 3,
        scratch_shapes=[
            pltpu.VMEM((ROWS, size), f32),
            pltpu.SMEM((ROWS,), f32),
            pltpu.VMEM((size // LANES, LANES), f32),
            pltpu.VMEM((n, ROWS, width), f32),
            pltpu.VMEM((n, 1, LANES), f32),
            pltpu.VMEM((m, 1, LANES), f32),
            pltpu.VMEM((m, ROWS, LANES), f32),
            pltpu.VMEM((m, ROWS, LANES), f32),
            pltpu.VMEM((m, 1, 2 * width + LANES), f32),
            pltpu.SemaphoreType.DMA((3,)),
            pltpu.SemaphoreType.DMA((5,)),
            pltpu.SemaphoreType.DMA((5,)),
        ],
        compiler_params=pltpu.CompilerParams(collective_id=0, has_side_effects=True),
    )(log_grads, local_energy, prev_update.reshape(size // LANES, LANES))
    rows, coeffs, update = pl.pallas_call(
        finish,
        out_shape=(
            jax.ShapeDtypeStruct((ROWS, LANES), f32),
            jax.ShapeDtypeStruct((ROWS,), f32),
            jax.ShapeDtypeStruct((size // LANES, LANES), f32),
        ),
        in_specs=[pl.BlockSpec(memory_space=pltpu.VMEM)] * 3,
        out_specs=[pl.BlockSpec(memory_space=pltpu.VMEM)] * 3,
    )(rows, coeffs, update)
    return rows, coeffs, update.reshape(size)


def plain(log_grads, local_energy, prev_update):
    high = lax.Precision.HIGHEST
    rows = log_grads.shape[0]
    count = rows * lax.axis_size("walker")
    col_sum, energy_sum = lax.psum((jnp.sum(log_grads, axis=0), jnp.sum(local_energy)), "walker")
    centered = (log_grads - col_sum / count) * count ** (-0.5)
    blocks = centered.astype(jnp.bfloat16)
    gathered = lax.all_gather(blocks, "walker", axis=0, tiled=True)
    kernel_rows = lax.dot_general(
        blocks, gathered, (((1,), (1,)), ((), ())), preferred_element_type=jnp.float32
    )
    target = -(local_energy - energy_sum / count) - momentum * jnp.dot(
        centered, prev_update, precision=high
    )
    coeffs = jnp.zeros_like(target)
    residual = target

    def squares(resid):
        return lax.psum(jnp.sum(resid * resid), "walker")

    direction = residual
    norm_now = squares(residual)
    for step in range(ITERS):
        full = lax.all_gather(direction, "walker", axis=0, tiled=True)
        image = jnp.dot(kernel_rows, full, precision=high) + damping * direction
        alpha = norm_now / lax.psum(jnp.sum(direction * image), "walker")
        coeffs = coeffs + alpha * direction
        if step + 1 < ITERS:
            residual = residual - alpha * image
            norm_next = squares(residual)
            direction = residual + norm_next / norm_now * direction
            norm_now = norm_next
    update = lax.psum(jnp.dot(coeffs, centered, precision=high), "walker") + momentum * prev_update
    return (kernel_rows, coeffs, update)


def local(log_grads, local_energy, prev_update):
    rows, columns = log_grads.shape
    n = lax.axis_size("walker")
    if rows == ROWS and n * ROWS == LANES and columns == n * LANES:
        return fused(log_grads, local_energy, prev_update)
    return plain(log_grads, local_energy, prev_update)


def solution(mesh):
    in_specs = (P(("groups", "walker"), None), P(("groups", "walker")), P("groups"))
    out_specs = (P(("groups", "walker"), None), P(("groups", "walker")), P("groups"))
    return jax.shard_map(local, mesh=mesh, in_specs=in_specs, out_specs=out_specs, check_vma=False)
```

```python
import functools

import jax
import jax.numpy as jnp
from jax import lax
from jax.experimental import pallas as pl
from jax.experimental.pallas import tpu as pltpu
from jax.sharding import PartitionSpec as P

ITERS = 2
LANES = 128
ROWS = 8
TEAM = 8
MESH = pl.DeviceIdType.MESH

momentum = 0.9
damping = 0.5


def kernel(
    n, m, x_hbm, e_hbm, p_hbm, rows_ref, coeffs_ref, update_ref,
    x_ref, e_ref, p_ref, tiles, w_rows, y_rows, k_send, k_recv, fin,
    in_sem, send_sem, recv_sem,
):
    walkers = n * ROWS
    width = tiles.shape[2]
    chunks = width // LANES
    scale = walkers ** (-0.5)
    group = lax.axis_index("groups")
    me = lax.axis_index("walker")
    pos = lax.rem(me, m)
    team = me - pos
    peers = [lax.rem(me + k, n) for k in range(1, n)]
    mates = [lax.rem(pos + k, m) for k in range(1, m)]

    barrier = pltpu.get_barrier_semaphore()
    for peer in peers[::-1]:
        pl.semaphore_signal(barrier, inc=1, device_id=(group, peer), device_id_type=MESH)
    loads = [
        pltpu.make_async_copy(x_hbm, x_ref, in_sem.at[0]),
        pltpu.make_async_copy(p_hbm, p_ref, in_sem.at[1]),
        pltpu.make_async_copy(e_hbm, e_ref, in_sem.at[2]),
    ]
    for load in loads:
        load.start()
    for load in loads:
        load.wait()

    def share(place):
        return pl.ds(pl.multiple_of(place * width, LANES), width)

    def remote(src, dst, which, peer):
        return pltpu.make_async_remote_copy(
            src_ref=src, dst_ref=dst, send_sem=send_sem.at[which], recv_sem=recv_sem.at[which],
            device_id=(group, peer), device_id_type=MESH,
        )

    def wait_all(ref, count, sem):
        if count:
            part = ref.at[pl.ds(0, count)]
            pltpu.make_async_copy(part, part, sem).wait()

    lane = lax.broadcasted_iota(jnp.int32, (1, LANES), 1)
    lane8 = lax.broadcasted_iota(jnp.int32, (ROWS, LANES), 1)
    sub8 = lax.broadcasted_iota(jnp.int32, (ROWS, LANES), 0)

    acc = jnp.zeros((ROWS, LANES), jnp.float32)
    for k in range(p_ref.shape[0]):
        acc = acc + x_ref[:, k * LANES : (k + 1) * LANES] * p_ref[k : k + 1, :]
    own = jnp.sum(acc, axis=1, keepdims=True) * (-momentum * scale)
    w_row = jnp.sum(jnp.where(lane8 == me * ROWS + sub8, own, 0.0), axis=0, keepdims=True)
    for i in range(ROWS):
        w_row = w_row - jnp.where(lane == me * ROWS + i, e_ref[i], 0.0)
    w_rows[me] = w_row
    tiles[me] = x_ref[:, share(pos)]

    pl.semaphore_wait(barrier, n - 1)
    for peer in peers:
        remote(w_rows.at[me], w_rows.at[me], 1, peer).start()
        remote(x_ref.at[:, share(lax.rem(peer, m))], tiles.at[me], 0, peer).start()

    sub = lax.broadcasted_iota(jnp.int32, (walkers, LANES), 0)
    lanes = lax.broadcasted_iota(jnp.int32, (walkers, LANES), 1)
    diagonal = sub == lanes

    def to_column(row):
        return jnp.sum(jnp.where(diagonal, row, 0.0), axis=1, keepdims=True)

    def to_row(column):
        return jnp.sum(jnp.where(diagonal, column, 0.0), axis=0, keepdims=True)

    def cols(c):
        return slice(c * LANES, (c + 1) * LANES)

    def rounded(c):
        return tiles[:, :, cols(c)].reshape(walkers, LANES).astype(jnp.bfloat16).astype(jnp.float32)

    wait_all(w_rows, n - 1, recv_sem.at[1])
    w = jnp.sum(w_rows[...], axis=0)
    t = w - jnp.sum(w, axis=1, keepdims=True) / walkers
    t_col = to_column(t)
    wait_all(tiles, n - 1, recv_sem.at[0])
    y_acc = jnp.zeros((walkers, LANES), jnp.float32)
    bt = []
    for c in range(chunks):
        x = tiles[:, :, cols(c)].reshape(walkers, LANES)
        centered = (x - jnp.sum(x, axis=0, keepdims=True) / walkers) * scale
        tiles[:, :, cols(c)] = centered.reshape(n, ROWS, LANES)
        blocks = centered.astype(jnp.bfloat16).astype(jnp.float32)
        bt.append(jnp.sum(blocks * t_col, axis=0, keepdims=True))
        y_acc = y_acc + blocks * bt[c]
    y_rows[pos] = to_row(jnp.sum(y_acc, axis=1, keepdims=True))
    for mate in mates:
        remote(y_rows.at[pos], y_rows.at[pos], 2, team + mate).start()

    half = tiles[...].reshape(walkers, width).astype(jnp.bfloat16)
    ours = tiles[pl.ds(team, m)].reshape(m * ROWS, width).astype(jnp.bfloat16)
    k_part = lax.dot_general(ours, half, (((1,), (1,)), ((), ())), preferred_element_type=jnp.float32)
    k_send[...] = k_part.reshape(m, ROWS, LANES)
    k_recv[pos] = k_send[pos]
    for mate in mates:
        remote(k_send.at[mate], k_recv.at[pos], 3, team + mate).start()
    ct = [
        jnp.sum(tiles[:, :, cols(c)].reshape(walkers, LANES) * t_col, axis=0, keepdims=True)
        for c in range(chunks)
    ]
    norm = jnp.sum(t * t, axis=1, keepdims=True)

    wait_all(y_rows, m - 1, recv_sem.at[2])
    image = jnp.sum(y_rows[...], axis=0) + damping * t
    i_col = to_column(image)
    alpha = norm / jnp.sum(t * image, axis=1, keepdims=True)
    residual = t - alpha * image
    norm_next = jnp.sum(residual * residual, axis=1, keepdims=True)
    beta = norm_next / norm
    direction = residual + beta * t
    squares = jnp.zeros((1, LANES), jnp.float32)
    for c in range(chunks):
        bi = jnp.sum(rounded(c) * i_col, axis=0, keepdims=True)
        ci = jnp.sum(tiles[:, :, cols(c)].reshape(walkers, LANES) * i_col, axis=0, keepdims=True)
        bd = (bt[c] - alpha * bi) + beta * bt[c]
        squares = squares + bd * bd
        fin[pos, :, cols(c)] = alpha * ct[c] + momentum * p_ref[pl.ds(pos * chunks + c, 1), :]
        fin[pos, :, cols(chunks + c)] = (ct[c] - alpha * ci) + beta * ct[c]
    fin[pos, :, cols(2 * chunks)] = squares
    for mate in mates:
        remote(fin.at[pos], fin.at[pos], 4, team + mate).start()

    square = jnp.sum(direction * direction, axis=1, keepdims=True)
    wait_all(k_recv, m - 1, recv_sem.at[3])
    rows_ref[...] = jnp.sum(k_recv[...], axis=0)

    wait_all(fin, m - 1, recv_sem.at[4])
    curve = jnp.sum(jnp.sum(fin[:, :, cols(2 * chunks)], axis=0), axis=1, keepdims=True)
    alpha2 = norm_next / (curve + damping * square)
    coeffs = alpha * t + alpha2 * direction
    coeffs_ref[...] = pltpu.roll(coeffs, lax.rem(walkers - me * ROWS, walkers), 1)
    for k in range(m * chunks):
        owner, c = k // chunks, k % chunks
        update_ref[k : k + 1, :] = fin[owner, :, cols(c)] + alpha2 * fin[owner, :, cols(chunks + c)]

    wait_all(tiles, n - 1, send_sem.at[0])
    wait_all(w_rows, n - 1, send_sem.at[1])
    wait_all(y_rows, m - 1, send_sem.at[2])
    wait_all(k_recv, m - 1, send_sem.at[3])
    wait_all(fin, m - 1, send_sem.at[4])


def finish(rows_in, coeffs_in, update_in, rows_ref, coeffs_ref, update_ref):
    rows_ref[...] = rows_in[...]
    coeffs_ref[...] = coeffs_in[0, 0:ROWS]
    update_ref[...] = update_in[...]


def fused(log_grads, local_energy, prev_update):
    n = lax.axis_size("walker")
    m = TEAM
    size = prev_update.shape[0]
    width = size // m
    f32 = jnp.float32
    rows, coeffs, update = pl.pallas_call(
        functools.partial(kernel, n, m),
        out_shape=(
            jax.ShapeDtypeStruct((ROWS, LANES), f32),
            jax.ShapeDtypeStruct((1, LANES), f32),
            jax.ShapeDtypeStruct((size // LANES, LANES), f32),
        ),
        in_specs=[pl.BlockSpec(memory_space=pl.ANY)] * 3,
        out_specs=[pl.BlockSpec(memory_space=pltpu.VMEM)] * 3,
        scratch_shapes=[
            pltpu.VMEM((ROWS, size), f32),
            pltpu.SMEM((ROWS,), f32),
            pltpu.VMEM((size // LANES, LANES), f32),
            pltpu.VMEM((n, ROWS, width), f32),
            pltpu.VMEM((n, 1, LANES), f32),
            pltpu.VMEM((m, 1, LANES), f32),
            pltpu.VMEM((m, ROWS, LANES), f32),
            pltpu.VMEM((m, ROWS, LANES), f32),
            pltpu.VMEM((m, 1, 2 * width + LANES), f32),
            pltpu.SemaphoreType.DMA((3,)),
            pltpu.SemaphoreType.DMA((5,)),
            pltpu.SemaphoreType.DMA((5,)),
        ],
        compiler_params=pltpu.CompilerParams(collective_id=0, has_side_effects=True),
    )(log_grads, local_energy, prev_update.reshape(size // LANES, LANES))
    rows, coeffs, update = pl.pallas_call(
        finish,
        out_shape=(
            jax.ShapeDtypeStruct((ROWS, LANES), f32),
            jax.ShapeDtypeStruct((ROWS,), f32),
            jax.ShapeDtypeStruct((size // LANES, LANES), f32),
        ),
        in_specs=[pl.BlockSpec(memory_space=pltpu.VMEM)] * 3,
        out_specs=[pl.BlockSpec(memory_space=pltpu.VMEM)] * 3,
    )(rows, coeffs, update)
    return rows, coeffs, update.reshape(size)


def plain(log_grads, local_energy, prev_update):
    high = lax.Precision.HIGHEST
    rows = log_grads.shape[0]
    count = rows * lax.axis_size("walker")
    col_sum, energy_sum = lax.psum((jnp.sum(log_grads, axis=0), jnp.sum(local_energy)), "walker")
    centered = (log_grads - col_sum / count) * count ** (-0.5)
    blocks = centered.astype(jnp.bfloat16)
    gathered = lax.all_gather(blocks, "walker", axis=0, tiled=True)
    kernel_rows = lax.dot_general(
        blocks, gathered, (((1,), (1,)), ((), ())), preferred_element_type=jnp.float32
    )
    target = -(local_energy - energy_sum / count) - momentum * jnp.dot(
        centered, prev_update, precision=high
    )
    coeffs = jnp.zeros_like(target)
    residual = target

    def squares(resid):
        return lax.psum(jnp.sum(resid * resid), "walker")

    direction = residual
    norm_now = squares(residual)
    for step in range(ITERS):
        full = lax.all_gather(direction, "walker", axis=0, tiled=True)
        image = jnp.dot(kernel_rows, full, precision=high) + damping * direction
        alpha = norm_now / lax.psum(jnp.sum(direction * image), "walker")
        coeffs = coeffs + alpha * direction
        if step + 1 < ITERS:
            residual = residual - alpha * image
            norm_next = squares(residual)
            direction = residual + norm_next / norm_now * direction
            norm_now = norm_next
    update = lax.psum(jnp.dot(coeffs, centered, precision=high), "walker") + momentum * prev_update
    return (kernel_rows, coeffs, update)


def local(log_grads, local_energy, prev_update):
    rows, columns = log_grads.shape
    n = lax.axis_size("walker")
    if rows == ROWS and n * ROWS == LANES and columns == n * LANES:
        return fused(log_grads, local_energy, prev_update)
    return plain(log_grads, local_energy, prev_update)


def solution(mesh):
    in_specs = (P(("groups", "walker"), None), P(("groups", "walker")), P("groups"))
    out_specs = (P(("groups", "walker"), None), P(("groups", "walker")), P("groups"))
    return jax.shard_map(local, mesh=mesh, in_specs=in_specs, out_specs=out_specs, check_vma=False)
```

```python
import functools

import jax
import jax.numpy as jnp
from jax import lax
from jax.experimental import pallas as pl
from jax.experimental.pallas import tpu as pltpu
from jax.sharding import PartitionSpec as P

ITERS = 2
LANES = 128
ROWS = 8
TEAM = 8
MESH = pl.DeviceIdType.MESH

momentum = 0.9
damping = 0.5


def kernel(
    n, m, x_hbm, e_hbm, p_hbm, rows_ref, coeffs_ref, update_ref,
    x_ref, e_ref, p_ref, tiles, w_rows, y_rows, k_send, k_recv, fin, first,
    in_sem, send_sem, recv_sem,
):
    walkers = n * ROWS
    width = tiles.shape[2]
    chunks = width // LANES
    scale = walkers ** (-0.5)
    group = lax.axis_index("groups")
    me = lax.axis_index("walker")
    pos = lax.rem(me, m)
    team = me - pos
    peers = [lax.rem(me + k, n) for k in range(1, n)]
    mates = [lax.rem(pos + k, m) for k in range(1, m)]

    barrier = pltpu.get_barrier_semaphore()
    for peer in peers[::-1]:
        pl.semaphore_signal(barrier, inc=1, device_id=(group, peer), device_id_type=MESH)
    loads = [
        pltpu.make_async_copy(x_hbm, x_ref, in_sem.at[0]),
        pltpu.make_async_copy(p_hbm, p_ref, in_sem.at[1]),
        pltpu.make_async_copy(e_hbm, e_ref, in_sem.at[2]),
    ]
    for load in loads:
        load.start()
    for load in loads:
        load.wait()

    def share(place):
        return pl.ds(pl.multiple_of(place * width, LANES), width)

    def remote(src, dst, which, peer):
        return pltpu.make_async_remote_copy(
            src_ref=src, dst_ref=dst, send_sem=send_sem.at[which], recv_sem=recv_sem.at[which],
            device_id=(group, peer), device_id_type=MESH,
        )

    def wait_all(ref, count, sem):
        if count:
            part = ref.at[pl.ds(0, count)]
            pltpu.make_async_copy(part, part, sem).wait()

    lane = lax.broadcasted_iota(jnp.int32, (1, LANES), 1)
    lane8 = lax.broadcasted_iota(jnp.int32, (ROWS, LANES), 1)
    sub8 = lax.broadcasted_iota(jnp.int32, (ROWS, LANES), 0)

    acc = jnp.zeros((ROWS, LANES), jnp.float32)
    for k in range(p_ref.shape[0]):
        acc = acc + x_ref[:, k * LANES : (k + 1) * LANES] * p_ref[k : k + 1, :]
    own = jnp.sum(acc, axis=1, keepdims=True) * (-momentum * scale)
    w_row = jnp.sum(jnp.where(lane8 == me * ROWS + sub8, own, 0.0), axis=0, keepdims=True)
    for i in range(ROWS):
        w_row = w_row - jnp.where(lane == me * ROWS + i, e_ref[i], 0.0)
    w_rows[me] = w_row
    tiles[me] = x_ref[:, share(pos)]

    pl.semaphore_wait(barrier, n - 1)
    for peer in peers:
        remote(w_rows.at[me], w_rows.at[me], 1, peer).start()
        remote(x_ref.at[:, share(lax.rem(peer, m))], tiles.at[me], 0, peer).start()

    sub = lax.broadcasted_iota(jnp.int32, (walkers, LANES), 0)
    lanes = lax.broadcasted_iota(jnp.int32, (walkers, LANES), 1)
    diagonal = sub == lanes

    def to_column(row):
        return jnp.sum(jnp.where(diagonal, row, 0.0), axis=1, keepdims=True)

    def to_row(column):
        return jnp.sum(jnp.where(diagonal, column, 0.0), axis=0, keepdims=True)

    def cols(c):
        return slice(c * LANES, (c + 1) * LANES)

    def rounded(c):
        return tiles[:, :, cols(c)].reshape(walkers, LANES).astype(jnp.bfloat16).astype(jnp.float32)

    wait_all(w_rows, n - 1, recv_sem.at[1])
    w = jnp.sum(w_rows[...], axis=0)
    t = w - jnp.sum(w, axis=1, keepdims=True) / walkers
    t_col = to_column(t)
    wait_all(tiles, n - 1, recv_sem.at[0])
    y_acc = jnp.zeros((walkers, LANES), jnp.float32)
    bt = []
    for c in range(chunks):
        x = tiles[:, :, cols(c)].reshape(walkers, LANES)
        centered = (x - jnp.sum(x, axis=0, keepdims=True) / walkers) * scale
        tiles[:, :, cols(c)] = centered.reshape(n, ROWS, LANES)
        blocks = centered.astype(jnp.bfloat16).astype(jnp.float32)
        bt.append(jnp.sum(blocks * t_col, axis=0, keepdims=True))
        y_acc = y_acc + blocks * bt[c]
    y_rows[pos] = to_row(jnp.sum(y_acc, axis=1, keepdims=True))
    for mate in mates:
        remote(y_rows.at[pos], y_rows.at[pos], 2, team + mate).start()

    half = tiles[...].reshape(walkers, width).astype(jnp.bfloat16)
    ours = tiles[pl.ds(team, m)].reshape(m * ROWS, width).astype(jnp.bfloat16)
    k_part = lax.dot_general(ours, half, (((1,), (1,)), ((), ())), preferred_element_type=jnp.float32)
    k_send[...] = k_part.reshape(m, ROWS, LANES)
    k_recv[pos] = k_send[pos]
    for mate in mates:
        remote(k_send.at[mate], k_recv.at[pos], 3, team + mate).start()
    ct = [
        jnp.sum(tiles[:, :, cols(c)].reshape(walkers, LANES) * t_col, axis=0, keepdims=True)
        for c in range(chunks)
    ]
    norm = jnp.sum(t * t, axis=1, keepdims=True)
    for c in range(chunks):
        first[pos, :, cols(c)] = ct[c]
    for mate in mates:
        remote(first.at[pos], first.at[pos], 5, team + mate).start()

    wait_all(y_rows, m - 1, recv_sem.at[2])
    image = jnp.sum(y_rows[...], axis=0) + damping * t
    i_col = to_column(image)
    alpha = norm / jnp.sum(t * image, axis=1, keepdims=True)
    residual = t - alpha * image
    norm_next = jnp.sum(residual * residual, axis=1, keepdims=True)
    beta = norm_next / norm
    direction = residual + beta * t
    squares = jnp.zeros((1, LANES), jnp.float32)
    for c in range(chunks):
        bi = jnp.sum(rounded(c) * i_col, axis=0, keepdims=True)
        ci = jnp.sum(tiles[:, :, cols(c)].reshape(walkers, LANES) * i_col, axis=0, keepdims=True)
        bd = (bt[c] - alpha * bi) + beta * bt[c]
        squares = squares + bd * bd
        fin[pos, :, cols(c)] = (ct[c] - alpha * ci) + beta * ct[c]
    fin[pos, :, cols(chunks)] = squares
    for mate in mates:
        remote(fin.at[pos], fin.at[pos], 4, team + mate).start()

    square = jnp.sum(direction * direction, axis=1, keepdims=True)
    wait_all(k_recv, m - 1, recv_sem.at[3])
    rows_ref[...] = jnp.sum(k_recv[...], axis=0)

    wait_all(first, m - 1, recv_sem.at[5])
    base = [
        alpha * first[k // chunks, :, cols(k % chunks)] + momentum * p_ref[k : k + 1, :]
        for k in range(m * chunks)
    ]
    wait_all(fin, m - 1, recv_sem.at[4])
    curve = jnp.sum(jnp.sum(fin[:, :, cols(chunks)], axis=0), axis=1, keepdims=True)
    alpha2 = norm_next / (curve + damping * square)
    coeffs = alpha * t + alpha2 * direction
    coeffs_ref[...] = pltpu.roll(coeffs, lax.rem(walkers - me * ROWS, walkers), 1)
    for k in range(m * chunks):
        owner, c = k // chunks, k % chunks
        update_ref[k : k + 1, :] = base[k] + alpha2 * fin[owner, :, cols(c)]

    wait_all(tiles, n - 1, send_sem.at[0])
    wait_all(w_rows, n - 1, send_sem.at[1])
    wait_all(y_rows, m - 1, send_sem.at[2])
    wait_all(k_recv, m - 1, send_sem.at[3])
    wait_all(fin, m - 1, send_sem.at[4])
    wait_all(first, m - 1, send_sem.at[5])


def finish(rows_in, coeffs_in, update_in, rows_ref, coeffs_ref, update_ref):
    rows_ref[...] = rows_in[...]
    coeffs_ref[...] = coeffs_in[0, 0:ROWS]
    update_ref[...] = update_in[...]


def fused(log_grads, local_energy, prev_update):
    n = lax.axis_size("walker")
    m = TEAM
    size = prev_update.shape[0]
    width = size // m
    f32 = jnp.float32
    rows, coeffs, update = pl.pallas_call(
        functools.partial(kernel, n, m),
        out_shape=(
            jax.ShapeDtypeStruct((ROWS, LANES), f32),
            jax.ShapeDtypeStruct((1, LANES), f32),
            jax.ShapeDtypeStruct((size // LANES, LANES), f32),
        ),
        in_specs=[pl.BlockSpec(memory_space=pl.ANY)] * 3,
        out_specs=[pl.BlockSpec(memory_space=pltpu.VMEM)] * 3,
        scratch_shapes=[
            pltpu.VMEM((ROWS, size), f32),
            pltpu.SMEM((ROWS,), f32),
            pltpu.VMEM((size // LANES, LANES), f32),
            pltpu.VMEM((n, ROWS, width), f32),
            pltpu.VMEM((n, 1, LANES), f32),
            pltpu.VMEM((m, 1, LANES), f32),
            pltpu.VMEM((m, ROWS, LANES), f32),
            pltpu.VMEM((m, ROWS, LANES), f32),
            pltpu.VMEM((m, 1, width + LANES), f32),
            pltpu.VMEM((m, 1, width), f32),
            pltpu.SemaphoreType.DMA((3,)),
            pltpu.SemaphoreType.DMA((6,)),
            pltpu.SemaphoreType.DMA((6,)),
        ],
        compiler_params=pltpu.CompilerParams(collective_id=0, has_side_effects=True),
    )(log_grads, local_energy, prev_update.reshape(size // LANES, LANES))
    rows, coeffs, update = pl.pallas_call(
        finish,
        out_shape=(
            jax.ShapeDtypeStruct((ROWS, LANES), f32),
            jax.ShapeDtypeStruct((ROWS,), f32),
            jax.ShapeDtypeStruct((size // LANES, LANES), f32),
        ),
        in_specs=[pl.BlockSpec(memory_space=pltpu.VMEM)] * 3,
        out_specs=[pl.BlockSpec(memory_space=pltpu.VMEM)] * 3,
    )(rows, coeffs, update)
    return rows, coeffs, update.reshape(size)


def plain(log_grads, local_energy, prev_update):
    high = lax.Precision.HIGHEST
    rows = log_grads.shape[0]
    count = rows * lax.axis_size("walker")
    col_sum, energy_sum = lax.psum((jnp.sum(log_grads, axis=0), jnp.sum(local_energy)), "walker")
    centered = (log_grads - col_sum / count) * count ** (-0.5)
    blocks = centered.astype(jnp.bfloat16)
    gathered = lax.all_gather(blocks, "walker", axis=0, tiled=True)
    kernel_rows = lax.dot_general(
        blocks, gathered, (((1,), (1,)), ((), ())), preferred_element_type=jnp.float32
    )
    target = -(local_energy - energy_sum / count) - momentum * jnp.dot(
        centered, prev_update, precision=high
    )
    coeffs = jnp.zeros_like(target)
    residual = target

    def squares(resid):
        return lax.psum(jnp.sum(resid * resid), "walker")

    direction = residual
    norm_now = squares(residual)
    for step in range(ITERS):
        full = lax.all_gather(direction, "walker", axis=0, tiled=True)
        image = jnp.dot(kernel_rows, full, precision=high) + damping * direction
        alpha = norm_now / lax.psum(jnp.sum(direction * image), "walker")
        coeffs = coeffs + alpha * direction
        if step + 1 < ITERS:
            residual = residual - alpha * image
            norm_next = squares(residual)
            direction = residual + norm_next / norm_now * direction
            norm_now = norm_next
    update = lax.psum(jnp.dot(coeffs, centered, precision=high), "walker") + momentum * prev_update
    return (kernel_rows, coeffs, update)


def local(log_grads, local_energy, prev_update):
    rows, columns = log_grads.shape
    n = lax.axis_size("walker")
    if rows == ROWS and n * ROWS == LANES and columns == n * LANES:
        return fused(log_grads, local_energy, prev_update)
    return plain(log_grads, local_energy, prev_update)


def solution(mesh):
    in_specs = (P(("groups", "walker"), None), P(("groups", "walker")), P("groups"))
    out_specs = (P(("groups", "walker"), None), P(("groups", "walker")), P("groups"))
    return jax.shard_map(local, mesh=mesh, in_specs=in_specs, out_specs=out_specs, check_vma=False)
```
